32 devices in a mesh: tm: 8 (over y, x, core), pts: 4 (over z).
Axes of the slice: x: 2, y: 2, z: 4, core: 2. Of those that a mesh axis runs over, the one named last changes fastest.
Arguments:
- snapshots: bfloat16 [16, 512, 5, 1024], P(None, 'tm', None, 'pts'), may hold values from -8 to 8
- weights: float32 [5, 1024], P(None, 'pts'), may hold values from 7.8125e-05 to 0.00078125
- freq_bins: int32 [64], replicated, may hold values from 0 to 255, as said below
- bin_owners: int32 [64], replicated, may hold values from 0 to 7, as said below
Outputs:
- csd: float32 [128, 512], P('tm')
The draws below stay inside these ranges and needn't reach their ends.
Inputs may be any that keep to these rules, and one draw needn't show every extreme that they name: `freq_bins`: the listed bins are distinct. `bin_owners`: no owner holds more than 16 listed bins and one holds exactly 16; owners hold uneven numbers of bins.
All inputs are finite; a program needn't handle non-finite values.
Results may differ from the reference program's by a relative error of at most 0.00053.
Values may be sent and summed in bfloat16 or wider, within the bound.
A program may use at most 64 MiB of HBM per device.

```python
import math
import jax
import jax.numpy as jnp
from jax import lax

NB = 16
NFFT = 512
NF = 5
CAP = 16
NK = 64
NP = 1024
N_TM = 8


def draw_snapshots(key, part):
    key_noise, key_common = jax.random.split(jax.random.fold_in(key, 11), 2)
    common = jax.random.normal(key_common, (1, NFFT, NF, NP), jnp.float32)
    noise = jax.random.normal(key_noise, (NB, NFFT, NF, NP), jnp.float32)
    values = noise + 0.8 * common
    return jnp.clip(values, -8.0, 8.0).astype(jnp.bfloat16)


def draw_freq_bins(key, part):
    order = jax.random.permutation(jax.random.fold_in(key, 23), NFFT // 2)
    return order[:NK].astype(jnp.int32)


def draw_bin_owners(key, part):
    key_order, key_share, key_shuffle = jax.random.split(jax.random.fold_in(key, 37), 3)
    half = N_TM // 2
    order = jax.random.permutation(key_order, N_TM).astype(jnp.int32)
    share = jax.random.randint(key_share, (half,), 0, CAP + 1).astype(jnp.int32)
    share = share.at[0].set(CAP)
    counts = jnp.zeros((N_TM,), jnp.int32).at[order[:half]].set(share).at[order[half:]].set(CAP - share)
    ends = jnp.cumsum(counts)
    sorted_owner = jnp.sum((jnp.arange(NK, dtype=jnp.int32)[:, None] >= ends[None, :]).astype(jnp.int32), axis=1)
    shuffle = jax.random.permutation(key_shuffle, NK)
    return sorted_owner[shuffle].astype(jnp.int32)


def block_levels(rng, dims, cuts, low, top_value):
    level = 1.0
    for axis_at, parts in cuts:
        steps = jax.random.uniform(jax.random.fold_in(jax.random.fold_in(rng, 6), axis_at), (parts,), jnp.float32, low / len(cuts), top_value / len(cuts))
        level = level * jnp.repeat(jnp.exp(steps), dims[axis_at] // parts).reshape((-1,) + (1,) * (len(dims) - 1 - axis_at))
    return level


def setup_inputs(seed: int = 0) -> dict:
    arg_keys = jax.random.split(jax.random.key(seed), 5)
    return {
        "snapshots": draw_snapshots(jax.random.fold_in(arg_keys[4], 71), 0),
        "weights": jnp.clip(jnp.exp(math.log(0.00078125) - 2.3025851 * jax.random.uniform(arg_keys[1], (NF, NP), jnp.float32) ** block_levels(arg_keys[1], (NF, NP), ((1, 4),), -0.2, 0.2)), 7.812499825377017e-05, 0.00078125),
        "freq_bins": draw_freq_bins(jax.random.fold_in(arg_keys[4], 71), 0),
        "bin_owners": draw_bin_owners(jax.random.fold_in(arg_keys[4], 71), 0),
    }


def slot_index(bin_owners, owner_count):
    owner_ids = jnp.arange(owner_count, dtype=jnp.int32)
    onehot = (bin_owners[:, None] == owner_ids[None, :]).astype(jnp.int32)
    before = jnp.cumsum(onehot, axis=0) - onehot
    position = lax.optimization_barrier(jnp.sum(before * onehot, axis=1))
    return (bin_owners * CAP + position).astype(jnp.int32)

def dft_rows(bin_values, live_mask, fft_len):
    steps_t = jnp.arange(fft_len, dtype=jnp.int32)
    wound = bin_values[:, None] * steps_t[None, :] % fft_len
    angles = 2.0 * jnp.pi * wound.astype(jnp.float32) / fft_len
    hann_window = 0.5 - 0.5 * jnp.cos(2.0 * jnp.pi * steps_t.astype(jnp.float32) / fft_len)
    scaled = hann_window / jnp.sqrt(jnp.float32(3.0 * fft_len / 8.0))
    scaled = scaled[None, :] * live_mask[:, None]
    cosine = (scaled * jnp.cos(angles)).astype(jnp.bfloat16)
    sine_rows = (-scaled * jnp.sin(angles)).astype(jnp.bfloat16)
    return jnp.stack([cosine, sine_rows], axis=1).reshape(-1, fft_len)

def fold_gram(gram_mat, blocks):
    real_part = gram_mat[..., :blocks, :blocks] + gram_mat[..., blocks:, blocks:]
    imag_part = gram_mat[..., :blocks, blocks:] - gram_mat[..., blocks:, :blocks]
    leading = gram_mat.shape[:-2]
    return jnp.concatenate([real_part.reshape(leading + (blocks * blocks,)), imag_part.reshape(leading + (blocks * blocks,))], axis=-1)

def reference(snapshots, weights, freq_bins, bin_owners):
    blocks, fft_len, fields, points = snapshots.shape
    columns = fields * points
    by_time = jnp.transpose(snapshots.reshape(blocks, fft_len, columns), (1, 0, 2)).reshape(fft_len, blocks * columns)
    weight_row = weights.reshape(columns)

    def one_group(group_bins):
        dft_table = dft_rows(group_bins, jnp.ones(group_bins.shape, jnp.float32), fft_len)
        spectra = jnp.dot(dft_table, by_time, preferred_element_type=jnp.float32).astype(jnp.bfloat16)
        spectra = spectra.reshape(-1, 2 * blocks, columns)
        weighted = (spectra.astype(jnp.float32) * weight_row).astype(jnp.bfloat16)
        gram_mat = jnp.einsum('gac,gbc->gab', spectra.astype(jnp.float32), weighted.astype(jnp.float32), precision=lax.Precision.HIGHEST)
        return fold_gram(gram_mat, blocks)
    group_csd = lax.map(one_group, freq_bins.reshape(-1, 8))
    bin_csd = group_csd.reshape(-1, 2 * blocks * blocks)
    slot_ids = slot_index(bin_owners, N_TM)
    result = jnp.zeros((N_TM * CAP, 2 * blocks * blocks), jnp.float32)
    return result.at[slot_ids].set(bin_csd)
```

```python
import jax
import jax.numpy as jnp
from jax import lax
from jax.sharding import PartitionSpec as P

CAP = 16


def slot_index(bin_owners, owner_count):
    owner_ids = jnp.arange(owner_count, dtype=jnp.int32)
    onehot = (bin_owners[:, None] == owner_ids[None, :]).astype(jnp.int32)
    before = jnp.cumsum(onehot, axis=0) - onehot
    position = jnp.sum(before * onehot, axis=1)
    return bin_owners * CAP + position


def dft_rows(bin_values, live_mask, fft_len):
    steps_t = jnp.arange(fft_len, dtype=jnp.int32)
    wound = bin_values[:, None] * steps_t[None, :] % fft_len
    angles = 2.0 * jnp.pi * wound.astype(jnp.float32) / fft_len
    hann_window = 0.5 - 0.5 * jnp.cos(2.0 * jnp.pi * steps_t.astype(jnp.float32) / fft_len)
    scaled = hann_window / jnp.sqrt(jnp.float32(3.0 * fft_len / 8.0))
    scaled = scaled[None, :] * live_mask[:, None]
    cosine = (scaled * jnp.cos(angles)).astype(jnp.bfloat16)
    sine_rows = (-scaled * jnp.sin(angles)).astype(jnp.bfloat16)
    return jnp.stack([cosine, sine_rows], axis=1).reshape(-1, fft_len)


def fold_gram(gram_mat, blocks):
    real_part = gram_mat[..., :blocks, :blocks] + gram_mat[..., blocks:, blocks:]
    imag_part = gram_mat[..., :blocks, blocks:] - gram_mat[..., blocks:, :blocks]
    leading = gram_mat.shape[:-2]
    return jnp.concatenate(
        [
            real_part.reshape(leading + (blocks * blocks,)),
            imag_part.reshape(leading + (blocks * blocks,)),
        ],
        axis=-1,
    )


def shards(snapshots, weights, freq_bins, bin_owners):
    blocks, local_steps, fields, points = snapshots.shape
    tm_count = lax.axis_size("tm")
    fft_len = local_steps * tm_count
    sub_points = points // tm_count
    slot_count = tm_count * CAP
    by_point = lax.all_to_all(snapshots, "tm", split_axis=3, concat_axis=1, tiled=True)
    by_point = by_point.reshape(blocks, fft_len, fields * sub_points)
    slot_ids = slot_index(bin_owners, tm_count)
    ones = jnp.ones(freq_bins.shape, jnp.float32)
    dft_table = dft_rows(freq_bins, ones, fft_len)
    spectra = jnp.einsum(
        "st,btc->sbc", dft_table, by_point, preferred_element_type=jnp.float32
    ).astype(jnp.bfloat16)
    spectra = spectra.reshape(freq_bins.shape[0], 2, blocks, fields * sub_points)
    me = lax.axis_index("tm")
    own = lax.dynamic_slice_in_dim(weights, me * sub_points, sub_points, axis=1).reshape(-1)
    spectra = spectra.reshape(freq_bins.shape[0], 2 * blocks, fields * sub_points)
    weighted = (spectra * own).astype(jnp.bfloat16)
    gram_mat = jnp.einsum("kac,kbc->kab", spectra, weighted, preferred_element_type=jnp.float32)
    partial_value = fold_gram(gram_mat, blocks)
    summed = lax.psum(partial_value, ("tm", "pts"))
    own_slots = me * CAP + jnp.arange(CAP, dtype=jnp.int32)
    matches = (own_slots[:, None] == slot_ids[None, :]).astype(jnp.float32)
    return jnp.dot(matches, summed, precision=lax.Precision.HIGHEST)


def solution(mesh):
    in_specs = (P(None, "tm", None, "pts"), P(None, "pts"), P(), P())
    out_specs = P("tm", None)
    return jax.shard_map(shards, mesh=mesh, in_specs=in_specs, out_specs=out_specs, check_vma=False)
```

```python
import functools

import jax
import jax.numpy as jnp
from jax import lax
from jax.experimental import pallas as pl
from jax.experimental.pallas import tpu as pltpu
from jax.sharding import PartitionSpec as P

CAP = 16
MESH = pl.DeviceIdType.MESH
LANES = 128
VMEM_BYTES = 40 * 1024 * 1024


def slot_index(bin_owners, owner_count):
    owner_ids = jnp.arange(owner_count, dtype=jnp.int32)
    onehot = (bin_owners[:, None] == owner_ids[None, :]).astype(jnp.int32)
    before = jnp.cumsum(onehot, axis=0) - onehot
    position = jnp.sum(before * onehot, axis=1)
    return bin_owners * CAP + position


def dft_rows(bin_values, fft_len):
    steps_t = jnp.arange(fft_len, dtype=jnp.int32)
    wound = bin_values[:, None] * steps_t[None, :] % fft_len
    angles = 2.0 * jnp.pi * wound.astype(jnp.float32) / fft_len
    hann_window = 0.5 - 0.5 * jnp.cos(2.0 * jnp.pi * steps_t.astype(jnp.float32) / fft_len)
    scaled = hann_window / jnp.sqrt(jnp.float32(3.0 * fft_len / 8.0))
    scaled = scaled[None, :]
    cosine = (scaled * jnp.cos(angles)).astype(jnp.bfloat16)
    sine_rows = (-scaled * jnp.sin(angles)).astype(jnp.bfloat16)
    return jnp.concatenate([cosine, sine_rows], axis=0)


def fold_gram(gram_mat, blocks):
    real_part = gram_mat[..., :blocks, :blocks] + gram_mat[..., blocks:, blocks:]
    imag_part = gram_mat[..., :blocks, blocks:] - gram_mat[..., blocks:, :blocks]
    leading = gram_mat.shape[:-2]
    return jnp.concatenate(
        [
            real_part.reshape(leading + (blocks * blocks,)),
            imag_part.reshape(leading + (blocks * blocks,)),
        ],
        axis=-1,
    )


def exchange_kernel(count, x_ref, table_ref, spec_ref, send, held, send_sem, recv_sem):
    blocks, fields, steps, points = x_ref.shape
    sub = points // count
    group = LANES // sub
    me = lax.axis_index("tm")
    barrier = pltpu.get_barrier_semaphore()
    for k in range(1, count):
        pl.semaphore_signal(
            barrier, inc=1, device_id={"tm": lax.rem(me + k, count)}, device_id_type=MESH
        )
    for tile in range(blocks * fields // group):
        rows = [x_ref[j // fields, j % fields] for j in range(tile * group, (tile + 1) * group)]
        for d in range(count):
            packed = jnp.concatenate([r[:, d * sub : (d + 1) * sub] for r in rows], axis=1)
            send[d, :, tile * LANES : (tile + 1) * LANES] = packed
    pl.semaphore_wait(barrier, count - 1)
    copies = []
    for k in range(1, count):
        peer = lax.rem(me + k, count)
        copy = pltpu.make_async_remote_copy(
            src_ref=send.at[peer],
            dst_ref=held.at[me],
            send_sem=send_sem.at[k],
            recv_sem=recv_sem.at[k],
            device_id={"tm": peer},
            device_id_type=MESH,
        )
        copy.start()
        copies.append(copy)
    held[me] = send[me]
    for k in range(1, count):
        source = lax.rem(me + count - k, count)
        pltpu.make_async_remote_copy(
            src_ref=send.at[source],
            dst_ref=held.at[source],
            send_sem=send_sem.at[k],
            recv_sem=recv_sem.at[k],
            device_id={"tm": source},
            device_id_type=MESH,
        ).wait_recv()
    columns = held.shape[2]
    width = LANES * (5 if (columns // LANES) % 5 == 0 else 1)
    for c in range(columns // width):
        part = held[:, :, c * width : (c + 1) * width].reshape(count * steps, width)
        out = jnp.dot(table_ref[...], part, preferred_element_type=jnp.float32)
        spec_ref[:, c * width : (c + 1) * width] = out.astype(jnp.bfloat16)
    for copy in copies:
        copy.wait_send()


def exchange(by_field, table, count):
    blocks, fields, steps, points = by_field.shape
    columns = blocks * fields * points // count
    return pl.pallas_call(
        functools.partial(exchange_kernel, count),
        out_shape=jax.ShapeDtypeStruct((table.shape[0], columns), jnp.bfloat16),
        in_specs=[pl.BlockSpec(memory_space=pltpu.VMEM)] * 2,
        out_specs=pl.BlockSpec(memory_space=pltpu.VMEM),
        scratch_shapes=[
            pltpu.VMEM((count, steps, columns), jnp.bfloat16),
            pltpu.VMEM((count, steps, columns), jnp.bfloat16),
            pltpu.SemaphoreType.DMA((count,)),
            pltpu.SemaphoreType.DMA((count,)),
        ],
        compiler_params=pltpu.CompilerParams(
            collective_id=0, has_side_effects=True, vmem_limit_bytes=VMEM_BYTES
        ),
    )(by_field, table)


def reduce_kernel(count, depth, part_ref, out_ref, first, second, s1, r1, s2, r2):
    me, here = lax.axis_index("tm"), lax.axis_index("pts")
    barrier = pltpu.get_barrier_semaphore()
    for k in range(1, count):
        pl.semaphore_signal(
            barrier, inc=1, device_id={"tm": lax.rem(me + k, count)}, device_id_type=MESH
        )
    for k in range(1, depth):
        pl.semaphore_signal(
            barrier, inc=1, device_id={"pts": lax.rem(here + k, depth)}, device_id_type=MESH
        )
    pl.semaphore_wait(barrier, count + depth - 2)

    def over(axis, position, size, source, dest, send_sem, recv_sem):
        copies = []
        for k in range(1, size):
            peer = lax.rem(position + k, size)
            copy = pltpu.make_async_remote_copy(
                src_ref=source(peer),
                dst_ref=dest.at[position],
                send_sem=send_sem.at[k],
                recv_sem=recv_sem.at[k],
                device_id={axis: peer},
                device_id_type=MESH,
            )
            copy.start()
            copies.append(copy)
        dest[position] = source(position)[...]
        for k in range(1, size):
            origin = lax.rem(position + size - k, size)
            pltpu.make_async_remote_copy(
                src_ref=source(origin),
                dst_ref=dest.at[origin],
                send_sem=send_sem.at[k],
                recv_sem=recv_sem.at[k],
                device_id={axis: origin},
                device_id_type=MESH,
            ).wait_recv()
        total = dest[0]
        for k in range(1, size):
            total = total + dest[k]
        for copy in copies:
            copy.wait_send()
        return total

    total = over("tm", me, count, lambda d: part_ref.at[d], first, s1, r1)
    out_ref[...] = total
    out_ref[...] = over("pts", here, depth, lambda d: out_ref, second, s2, r2)


def reduce_slots(part, count, depth):
    cap, width = part.shape[1:]
    return pl.pallas_call(
        functools.partial(reduce_kernel, count, depth),
        out_shape=jax.ShapeDtypeStruct((cap, width), jnp.float32),
        in_specs=[pl.BlockSpec(memory_space=pltpu.VMEM)],
        out_specs=pl.BlockSpec(memory_space=pltpu.VMEM),
        scratch_shapes=[
            pltpu.VMEM((count, cap, width), jnp.float32),
            pltpu.VMEM((depth, cap, width), jnp.float32),
            pltpu.SemaphoreType.DMA((count,)),
            pltpu.SemaphoreType.DMA((count,)),
            pltpu.SemaphoreType.DMA((depth,)),
            pltpu.SemaphoreType.DMA((depth,)),
        ],
        compiler_params=pltpu.CompilerParams(
            collective_id=1, has_side_effects=True, vmem_limit_bytes=VMEM_BYTES
        ),
    )(part)


def shards(snapshots, weights, freq_bins, bin_owners):
    blocks, local_steps, fields, points = snapshots.shape
    tm_count = lax.axis_size("tm")
    pts_count = lax.axis_size("pts")
    listed = freq_bins.shape[0]
    sub_points = points // tm_count
    slot_count = tm_count * CAP
    table = dft_rows(freq_bins, local_steps * tm_count)
    spectra = exchange(jnp.transpose(snapshots, (0, 2, 1, 3)), table, tm_count)
    spectra = spectra.reshape(2, listed, blocks, fields * sub_points)
    me = lax.axis_index("tm")
    own = lax.dynamic_slice_in_dim(weights, me * sub_points, sub_points, axis=1).reshape(-1)
    spectra = jnp.transpose(spectra, (1, 0, 2, 3)).reshape(listed, 2 * blocks, -1)
    weighted = (spectra * own).astype(jnp.bfloat16)
    gram_mat = jnp.einsum("kac,kbc->kab", spectra, weighted, preferred_element_type=jnp.float32)
    partial_value = fold_gram(gram_mat, blocks)
    slot_ids = slot_index(bin_owners, tm_count)
    matches = slot_ids[None, :] == jnp.arange(slot_count, dtype=jnp.int32)[:, None]
    placed = jnp.dot(
        matches.astype(jnp.float32), partial_value, precision=lax.Precision.HIGHEST
    )
    return reduce_slots(placed.reshape(tm_count, CAP, -1), tm_count, pts_count)


def solution(mesh):
    in_specs = (P(None, "tm", None, "pts"), P(None, "pts"), P(), P())
    out_specs = P("tm", None)
    return jax.shard_map(shards, mesh=mesh, in_specs=in_specs, out_specs=out_specs, check_vma=False)
```

```python
import functools

import jax
import jax.numpy as jnp
from jax import lax
from jax.experimental import pallas as pl
from jax.experimental.pallas import tpu as pltpu
from jax.sharding import PartitionSpec as P

CAP = 16
MESH = pl.DeviceIdType.MESH
LANES = 128
VMEM_BYTES = 40 * 1024 * 1024


def slot_index(bin_owners, owner_count):
    owner_ids = jnp.arange(owner_count, dtype=jnp.int32)
    onehot = (bin_owners[:, None] == owner_ids[None, :]).astype(jnp.int32)
    before = jnp.cumsum(onehot, axis=0) - onehot
    position = jnp.sum(before * onehot, axis=1)
    return bin_owners * CAP + position


def dft_rows(bin_values, fft_len):
    steps_t = jnp.arange(fft_len, dtype=jnp.int32)
    wound = bin_values[:, None] * steps_t[None, :] % fft_len
    angles = 2.0 * jnp.pi * wound.astype(jnp.float32) / fft_len
    hann_window = 0.5 - 0.5 * jnp.cos(2.0 * jnp.pi * steps_t.astype(jnp.float32) / fft_len)
    scaled = hann_window / jnp.sqrt(jnp.float32(3.0 * fft_len / 8.0))
    scaled = scaled[None, :]
    cosine = (scaled * jnp.cos(angles)).astype(jnp.bfloat16)
    sine_rows = (-scaled * jnp.sin(angles)).astype(jnp.bfloat16)
    return jnp.concatenate([cosine, sine_rows], axis=0)


def fold_gram(gram_mat, blocks):
    real_part = gram_mat[..., :blocks, :blocks] + gram_mat[..., blocks:, blocks:]
    imag_part = gram_mat[..., :blocks, blocks:] - gram_mat[..., blocks:, :blocks]
    leading = gram_mat.shape[:-2]
    return jnp.concatenate(
        [
            real_part.reshape(leading + (blocks * blocks,)),
            imag_part.reshape(leading + (blocks * blocks,)),
        ],
        axis=-1,
    )


def exchange_kernel(count, x_ref, table_ref, spec_ref, send, held, send_sem, recv_sem):
    blocks, fields, steps, points = x_ref.shape
    sub = points // count
    group = LANES // sub
    me = lax.axis_index("tm")
    barrier = pltpu.get_barrier_semaphore()
    for k in range(1, count):
        pl.semaphore_signal(
            barrier, inc=1, device_id={"tm": lax.rem(me + k, count)}, device_id_type=MESH
        )
    chunks, width = send.shape[0], send.shape[3]
    per_chunk = width // LANES
    copies = []
    for c in range(chunks):
        for tile in range(per_chunk):
            first = (c * per_chunk + tile) * group
            rows = [x_ref[j // fields, j % fields] for j in range(first, first + group)]
            for d in range(count):
                packed = jnp.concatenate([r[:, d * sub : (d + 1) * sub] for r in rows], axis=1)
                send[c, d, :, tile * LANES : (tile + 1) * LANES] = packed
        if c == 0:
            pl.semaphore_wait(barrier, count - 1)
        for k in range(1, count):
            peer = lax.rem(me + k, count)
            copy = pltpu.make_async_remote_copy(
                src_ref=send.at[c, peer],
                dst_ref=held.at[c, me],
                send_sem=send_sem.at[c, k],
                recv_sem=recv_sem.at[c, k],
                device_id={"tm": peer},
                device_id_type=MESH,
            )
            copy.start()
            copies.append(copy)
        held[c, me] = send[c, me]
    for c in range(chunks):
        for k in range(1, count):
            source = lax.rem(me + count - k, count)
            pltpu.make_async_remote_copy(
                src_ref=send.at[c, source],
                dst_ref=held.at[c, source],
                send_sem=send_sem.at[c, k],
                recv_sem=recv_sem.at[c, k],
                device_id={"tm": source},
                device_id_type=MESH,
            ).wait_recv()
        part = held[c].reshape(count * steps, width)
        out = jnp.dot(table_ref[...], part, preferred_element_type=jnp.float32)
        spec_ref[:, c * width : (c + 1) * width] = out.astype(jnp.bfloat16)
    for copy in copies:
        copy.wait_send()


def exchange(by_field, table, count):
    blocks, fields, steps, points = by_field.shape
    columns = blocks * fields * points // count
    tiles = columns // LANES
    chunks = tiles // fields if tiles % fields == 0 else 1
    buffer = pltpu.VMEM((chunks, count, steps, columns // chunks), jnp.bfloat16)
    return pl.pallas_call(
        functools.partial(exchange_kernel, count),
        out_shape=jax.ShapeDtypeStruct((table.shape[0], columns), jnp.bfloat16),
        in_specs=[pl.BlockSpec(memory_space=pltpu.VMEM)] * 2,
        out_specs=pl.BlockSpec(memory_space=pltpu.VMEM),
        scratch_shapes=[
            buffer,
            buffer,
            pltpu.SemaphoreType.DMA((chunks, count)),
            pltpu.SemaphoreType.DMA((chunks, count)),
        ],
        compiler_params=pltpu.CompilerParams(
            collective_id=0, has_side_effects=True, vmem_limit_bytes=VMEM_BYTES
        ),
    )(by_field, table)


def reduce_kernel(count, depth, part_ref, out_ref, first, second, s1, r1, s2, r2):
    me, here = lax.axis_index("tm"), lax.axis_index("pts")
    barrier = pltpu.get_barrier_semaphore()
    for k in range(1, count):
        pl.semaphore_signal(
            barrier, inc=1, device_id={"tm": lax.rem(me + k, count)}, device_id_type=MESH
        )
    for k in range(1, depth):
        pl.semaphore_signal(
            barrier, inc=1, device_id={"pts": lax.rem(here + k, depth)}, device_id_type=MESH
        )
    pl.semaphore_wait(barrier, count + depth - 2)

    def over(axis, position, size, source, dest, send_sem, recv_sem):
        copies = []
        for k in range(1, size):
            peer = lax.rem(position + k, size)
            copy = pltpu.make_async_remote_copy(
                src_ref=source(peer),
                dst_ref=dest.at[position],
                send_sem=send_sem.at[k],
                recv_sem=recv_sem.at[k],
                device_id={axis: peer},
                device_id_type=MESH,
            )
            copy.start()
            copies.append(copy)
        dest[position] = source(position)[...]
        for k in range(1, size):
            origin = lax.rem(position + size - k, size)
            pltpu.make_async_remote_copy(
                src_ref=source(origin),
                dst_ref=dest.at[origin],
                send_sem=send_sem.at[k],
                recv_sem=recv_sem.at[k],
                device_id={axis: origin},
                device_id_type=MESH,
            ).wait_recv()
        total = dest[0]
        for k in range(1, size):
            total = total + dest[k]
        for copy in copies:
            copy.wait_send()
        return total

    total = over("tm", me, count, lambda d: part_ref.at[d], first, s1, r1)
    out_ref[...] = total
    out_ref[...] = over("pts", here, depth, lambda d: out_ref, second, s2, r2)


def reduce_slots(part, count, depth):
    cap, width = part.shape[1:]
    return pl.pallas_call(
        functools.partial(reduce_kernel, count, depth),
        out_shape=jax.ShapeDtypeStruct((cap, width), jnp.float32),
        in_specs=[pl.BlockSpec(memory_space=pltpu.VMEM)],
        out_specs=pl.BlockSpec(memory_space=pltpu.VMEM),
        scratch_shapes=[
            pltpu.VMEM((count, cap, width), jnp.float32),
            pltpu.VMEM((depth, cap, width), jnp.float32),
            pltpu.SemaphoreType.DMA((count,)),
            pltpu.SemaphoreType.DMA((count,)),
            pltpu.SemaphoreType.DMA((depth,)),
            pltpu.SemaphoreType.DMA((depth,)),
        ],
        compiler_params=pltpu.CompilerParams(
            collective_id=1, has_side_effects=True, vmem_limit_bytes=VMEM_BYTES
        ),
    )(part)


def shards(snapshots, weights, freq_bins, bin_owners):
    blocks, local_steps, fields, points = snapshots.shape
    tm_count = lax.axis_size("tm")
    pts_count = lax.axis_size("pts")
    listed = freq_bins.shape[0]
    sub_points = points // tm_count
    slot_count = tm_count * CAP
    table = dft_rows(freq_bins, local_steps * tm_count)
    spectra = exchange(jnp.transpose(snapshots, (0, 2, 1, 3)), table, tm_count)
    spectra = spectra.reshape(2, listed, blocks, fields * sub_points)
    me = lax.axis_index("tm")
    own = lax.dynamic_slice_in_dim(weights, me * sub_points, sub_points, axis=1).reshape(-1)
    spectra = jnp.transpose(spectra, (1, 0, 2, 3)).reshape(listed, 2 * blocks, -1)
    weighted = (spectra * own).astype(jnp.bfloat16)
    gram_mat = jnp.einsum("kac,kbc->kab", spectra, weighted, preferred_element_type=jnp.float32)
    partial_value = fold_gram(gram_mat, blocks)
    slot_ids = slot_index(bin_owners, tm_count)
    matches = slot_ids[None, :] == jnp.arange(slot_count, dtype=jnp.int32)[:, None]
    placed = jnp.dot(
        matches.astype(jnp.float32), partial_value, precision=lax.Precision.HIGHEST
    )
    return reduce_slots(placed.reshape(tm_count, CAP, -1), tm_count, pts_count)


def solution(mesh):
    in_specs = (P(None, "tm", None, "pts"), P(None, "pts"), P(), P())
    out_specs = P("tm", None)
    return jax.shard_map(shards, mesh=mesh, in_specs=in_specs, out_specs=out_specs, check_vma=False)
```

```python
import functools

import jax
import jax.numpy as jnp
from jax import lax
from jax.experimental import pallas as pl
from jax.experimental.pallas import tpu as pltpu
from jax.sharding import PartitionSpec as P

CAP = 16
MESH = pl.DeviceIdType.MESH
LANES = 128
VMEM_BYTES = 40 * 1024 * 1024
EXCHANGE_VMEM_BYTES = 60 * 1024 * 1024


def slot_index(bin_owners, owner_count):
    owner_ids = jnp.arange(owner_count, dtype=jnp.int32)
    onehot = (bin_owners[:, None] == owner_ids[None, :]).astype(jnp.int32)
    before = jnp.cumsum(onehot, axis=0) - onehot
    position = jnp.sum(before * onehot, axis=1)
    return bin_owners * CAP + position


def dft_rows(bin_values, fft_len):
    steps_t = jnp.arange(fft_len, dtype=jnp.int32)
    wound = bin_values[:, None] * steps_t[None, :] % fft_len
    angles = 2.0 * jnp.pi * wound.astype(jnp.float32) / fft_len
    hann_window = 0.5 - 0.5 * jnp.cos(2.0 * jnp.pi * steps_t.astype(jnp.float32) / fft_len)
    scaled = hann_window / jnp.sqrt(jnp.float32(3.0 * fft_len / 8.0))
    scaled = scaled[None, :]
    cosine = (scaled * jnp.cos(angles)).astype(jnp.bfloat16)
    sine_rows = (-scaled * jnp.sin(angles)).astype(jnp.bfloat16)
    return jnp.concatenate([cosine, sine_rows], axis=0)


def fold_gram(gram_mat, blocks):
    real_part = gram_mat[..., :blocks, :blocks] + gram_mat[..., blocks:, blocks:]
    imag_part = gram_mat[..., :blocks, blocks:] - gram_mat[..., blocks:, :blocks]
    leading = gram_mat.shape[:-2]
    return jnp.concatenate(
        [
            real_part.reshape(leading + (blocks * blocks,)),
            imag_part.reshape(leading + (blocks * blocks,)),
        ],
        axis=-1,
    )


def exchange_kernel(
    count, x_hbm, table_ref, spec_ref, x_ref, send, held, load_sem, send_sem, recv_sem
):
    blocks, fields, steps, points = x_ref.shape
    sub = points // count
    group = LANES // sub
    me = lax.axis_index("tm")
    loads = []
    rows_each = blocks // send.shape[0]
    for c in range(send.shape[0]):
        load = pltpu.make_async_copy(
            x_hbm.at[pl.ds(c * rows_each, rows_each)],
            x_ref.at[pl.ds(c * rows_each, rows_each)],
            load_sem.at[c],
        )
        load.start()
        loads.append(load)
    barrier = pltpu.get_barrier_semaphore()
    for k in range(1, count):
        pl.semaphore_signal(
            barrier, inc=1, device_id={"tm": lax.rem(me + k, count)}, device_id_type=MESH
        )
    chunks, width = send.shape[0], send.shape[3]
    per_chunk = width // LANES
    copies = []
    for c in range(chunks):
        loads[c].wait()
        for tile in range(per_chunk):
            first = (c * per_chunk + tile) * group
            rows = [x_ref[j // fields, j % fields] for j in range(first, first + group)]
            for d in range(count):
                packed = jnp.concatenate([r[:, d * sub : (d + 1) * sub] for r in rows], axis=1)
                send[c, d, :, tile * LANES : (tile + 1) * LANES] = packed
        if c == 0:
            pl.semaphore_wait(barrier, count - 1)
        for k in range(1, count):
            peer = lax.rem(me + k, count)
            copy = pltpu.make_async_remote_copy(
                src_ref=send.at[c, peer],
                dst_ref=held.at[c, me],
                send_sem=send_sem.at[c, k],
                recv_sem=recv_sem.at[c, k],
                device_id={"tm": peer},
                device_id_type=MESH,
            )
            copy.start()
            copies.append(copy)
        held[c, me] = send[c, me]
    for c in range(chunks):
        for k in range(1, count):
            source = lax.rem(me + count - k, count)
            pltpu.make_async_remote_copy(
                src_ref=send.at[c, source],
                dst_ref=held.at[c, source],
                send_sem=send_sem.at[c, k],
                recv_sem=recv_sem.at[c, k],
                device_id={"tm": source},
                device_id_type=MESH,
            ).wait_recv()
        part = held[c].reshape(count * steps, width)
        out = jnp.dot(table_ref[...], part, preferred_element_type=jnp.float32)
        spec_ref[:, c * width : (c + 1) * width] = out.astype(jnp.bfloat16)
    for copy in copies:
        copy.wait_send()


def exchange(by_field, table, count):
    blocks, fields, steps, points = by_field.shape
    columns = blocks * fields * points // count
    tiles = columns // LANES
    chunks = tiles // fields if tiles % fields == 0 else 1
    buffer = pltpu.VMEM((chunks, count, steps, columns // chunks), jnp.bfloat16)
    return pl.pallas_call(
        functools.partial(exchange_kernel, count),
        out_shape=jax.ShapeDtypeStruct((table.shape[0], columns), jnp.bfloat16),
        in_specs=[
            pl.BlockSpec(memory_space=pl.ANY),
            pl.BlockSpec(memory_space=pltpu.VMEM),
        ],
        out_specs=pl.BlockSpec(memory_space=pltpu.VMEM),
        scratch_shapes=[
            pltpu.VMEM(by_field.shape, jnp.bfloat16),
            buffer,
            buffer,
            pltpu.SemaphoreType.DMA((chunks,)),
            pltpu.SemaphoreType.DMA((chunks, count)),
            pltpu.SemaphoreType.DMA((chunks, count)),
        ],
        compiler_params=pltpu.CompilerParams(
            collective_id=0, has_side_effects=True, vmem_limit_bytes=EXCHANGE_VMEM_BYTES
        ),
    )(by_field, table)


def reduce_kernel(count, depth, part_ref, out_ref, first, second, s1, r1, s2, r2):
    me, here = lax.axis_index("tm"), lax.axis_index("pts")
    barrier = pltpu.get_barrier_semaphore()
    for k in range(1, count):
        pl.semaphore_signal(
            barrier, inc=1, device_id={"tm": lax.rem(me + k, count)}, device_id_type=MESH
        )
    for k in range(1, depth):
        pl.semaphore_signal(
            barrier, inc=1, device_id={"pts": lax.rem(here + k, depth)}, device_id_type=MESH
        )
    pl.semaphore_wait(barrier, count + depth - 2)

    def over(axis, position, size, source, dest, send_sem, recv_sem):
        copies = []
        for k in range(1, size):
            peer = lax.rem(position + k, size)
            copy = pltpu.make_async_remote_copy(
                src_ref=source(peer),
                dst_ref=dest.at[position],
                send_sem=send_sem.at[k],
                recv_sem=recv_sem.at[k],
                device_id={axis: peer},
                device_id_type=MESH,
            )
            copy.start()
            copies.append(copy)
        dest[position] = source(position)[...]
        for k in range(1, size):
            origin = lax.rem(position + size - k, size)
            pltpu.make_async_remote_copy(
                src_ref=source(origin),
                dst_ref=dest.at[origin],
                send_sem=send_sem.at[k],
                recv_sem=recv_sem.at[k],
                device_id={axis: origin},
                device_id_type=MESH,
            ).wait_recv()
        total = dest[0]
        for k in range(1, size):
            total = total + dest[k]
        for copy in copies:
            copy.wait_send()
        return total

    total = over("tm", me, count, lambda d: part_ref.at[d], first, s1, r1)
    out_ref[...] = total
    out_ref[...] = over("pts", here, depth, lambda d: out_ref, second, s2, r2)


def reduce_slots(part, count, depth):
    cap, width = part.shape[1:]
    return pl.pallas_call(
        functools.partial(reduce_kernel, count, depth),
        out_shape=jax.ShapeDtypeStruct((cap, width), jnp.float32),
        in_specs=[pl.BlockSpec(memory_space=pltpu.VMEM)],
        out_specs=pl.BlockSpec(memory_space=pltpu.VMEM),
        scratch_shapes=[
            pltpu.VMEM((count, cap, width), jnp.float32),
            pltpu.VMEM((depth, cap, width), jnp.float32),
            pltpu.SemaphoreType.DMA((count,)),
            pltpu.SemaphoreType.DMA((count,)),
            pltpu.SemaphoreType.DMA((depth,)),
            pltpu.SemaphoreType.DMA((depth,)),
        ],
        compiler_params=pltpu.CompilerParams(
            collective_id=1, has_side_effects=True, vmem_limit_bytes=VMEM_BYTES
        ),
    )(part)


def shards(snapshots, weights, freq_bins, bin_owners):
    blocks, local_steps, fields, points = snapshots.shape
    tm_count = lax.axis_size("tm")
    pts_count = lax.axis_size("pts")
    listed = freq_bins.shape[0]
    sub_points = points // tm_count
    slot_count = tm_count * CAP
    table = dft_rows(freq_bins, local_steps * tm_count)
    spectra = exchange(jnp.transpose(snapshots, (0, 2, 1, 3)), table, tm_count)
    spectra = spectra.reshape(2, listed, blocks, fields * sub_points)
    me = lax.axis_index("tm")
    own = lax.dynamic_slice_in_dim(weights, me * sub_points, sub_points, axis=1).reshape(-1)
    spectra = jnp.transpose(spectra, (1, 0, 2, 3)).reshape(listed, 2 * blocks, -1)
    weighted = (spectra * own).astype(jnp.bfloat16)
    gram_mat = jnp.einsum("kac,kbc->kab", spectra, weighted, preferred_element_type=jnp.float32)
    partial_value = fold_gram(gram_mat, blocks)
    slot_ids = slot_index(bin_owners, tm_count)
    matches = slot_ids[None, :] == jnp.arange(slot_count, dtype=jnp.int32)[:, None]
    placed = jnp.dot(
        matches.astype(jnp.float32), partial_value, precision=lax.Precision.HIGHEST
    )
    return reduce_slots(placed.reshape(tm_count, CAP, -1), tm_count, pts_count)


def solution(mesh):
    in_specs = (P(None, "tm", None, "pts"), P(None, "pts"), P(), P())
    out_specs = P("tm", None)
    return jax.shard_map(shards, mesh=mesh, in_specs=in_specs, out_specs=out_specs, check_vma=False)
```
